128 devices in a mesh: real: 4 (over y), cell: 32 (over z, x, core).
Axes of the slice: x: 4, y: 4, z: 4, core: 2. Of those that a mesh axis runs over, the one named last changes fastest.
Arguments:
- snapshots: bfloat16 [8, 2, 256, 65536], P('real', None, None, 'cell'), may hold values from -6 to 6
- quad_weights: int32 [65536], P('cell'), may hold values from 1 to 11
- triad_pairs: int32 [512, 2], replicated, may hold values from 1 to 62, as said below
- owner_counts: int32 [32], replicated, may hold values from 1 to 32, 512 in all
Outputs:
- bispectra: float32 [1024, 8, 8, 2], P('cell', 'real')
The draws below stay inside these ranges and needn't reach their ends.
Inputs may be any that keep to these rules, and one draw needn't show every extreme that they name: `owner_counts`: the counts sum to 512, each is at least 1, and the largest is exactly 32. `triad_pairs`: for each triad k >= 1, l >= 1 and k + l <= 63.
All inputs are finite; a program needn't handle non-finite values.
Results may differ from the reference program's by a relative error of at most 0.0075.
Values may be sent and summed in bfloat16 or wider, within the bound.
No kernel may reach another device: no remote copies, remote signals or barrier semaphores. Data moves between devices by JAX's collectives and lax.ppermute only.
A program may use at most 64 MiB of HBM per device.

```python
import math
import jax
import jax.numpy as jnp
import numpy as np
from jax import lax

SNAPS = 256
FREQS = 64
VARS = 2
TRI_DEV = 16
OWN_MOST = 32
REALS = 8
CELLS = 65536
TRIADS = 512
SLOTS = 1024
N_CELL = 32


def draw_triad_pairs(key, part):
    key = jax.random.fold_in(key, 11)
    first_key, second_key = jax.random.split(key)
    first_freq = jax.random.randint(first_key, (TRIADS,), 1, FREQS - 1)
    spread = jax.random.randint(second_key, (TRIADS,), 0, 1 << 20)
    second_freq = 1 + spread % (FREQS - 1 - first_freq)
    return jnp.stack([first_freq, second_freq], axis=1).astype(jnp.int32)


def draw_quad_weights(key, part):
    key = jax.random.fold_in(key, 5)
    base_weight = jax.random.randint(key, (CELLS,), 1, 6)
    positions = jnp.arange(CELLS, dtype=jnp.int32)
    return (base_weight + 7 * positions // CELLS).astype(jnp.int32)


def steps_of(own_key, shape, cuts, low, top_value):
    loudness, own = 1.0, jax.random.fold_in(own_key, 6)
    for axis_at, blocks in cuts:
        draws = jnp.exp(jax.random.uniform(jax.random.fold_in(own, axis_at), (blocks,), jnp.float32, low / len(cuts), top_value / len(cuts)))
        loudness = loudness * jnp.repeat(draws, shape[axis_at] // blocks).reshape([-1 if axis == axis_at else 1 for axis in range(len(shape))])
    return loudness


def length_profile(count, total, reach, skew):
    weights = [(1 << 20) // math.isqrt(rank ** skew) + 1 for rank in range(2, count + 1)]
    rest, given = total - reach - (count - 1), [1] * (count - 1)
    while rest > 0:
        movable = [i for i in range(count - 1) if given[i] < reach]
        whole, budget = sum([weights[i] for i in movable]), rest
        for i in movable:
            extra = min(reach - given[i], max(1, budget * weights[i] // whole), rest)
            given[i] = given[i] + extra
            rest = rest - extra
    return np.array([reach] + given)


def ragged_sizes(stream_key, amount, total, limit, lean):
    if amount == 2:
        one = jax.random.randint(stream_key, (), max(1, total - limit), min(limit, total - 1) + 1)
        return jnp.stack([one, total - one])
    tallies = jnp.asarray(length_profile(amount, total, limit, lean), jnp.int32)
    twos = (amount - 1) // 2
    giver, taker = tallies[1:1 + 2 * twos:2], tallies[2:2 + 2 * twos:2]
    margin = jnp.minimum(giver - 1, limit - taker)
    moved = jax.random.randint(jax.random.fold_in(stream_key, 1), (twos,), 0, 1 << 20) % (margin + 1)
    tallies = tallies.at[1:1 + 2 * twos:2].set(giver - moved).at[2:2 + 2 * twos:2].set(taker + moved)
    return tallies[jax.random.permutation(jax.random.fold_in(stream_key, 2), amount)]


def centred(own_key, extent, scale, most, pieces=(), kind=jnp.bfloat16):
    entries = jax.random.normal(own_key, extent, jnp.float32) * scale
    if len(pieces) > 0:
        entries = steps_of(own_key, extent, pieces, -0.22, 0.18) * entries
    return jnp.clip(entries, min=-most, max=most).astype(kind)


def setup_inputs(seed: int = 0) -> dict:
    seeds = jax.random.split(jax.random.key(seed), 5)
    return {
        "snapshots": centred(seeds[0], (REALS, VARS, SNAPS, CELLS), 1.0, 6.0, ((0, 4), (3, 32))),
        "quad_weights": draw_quad_weights(jax.random.fold_in(seeds[4], 71), 0),
        "triad_pairs": draw_triad_pairs(jax.random.fold_in(seeds[4], 71), 0),
        "owner_counts": ragged_sizes(seeds[3], N_CELL, TRIADS, OWN_MOST, 2).astype(jnp.int32),
    }


def dft_table(steps_total, freq_total):
    times = jnp.arange(steps_total, dtype=jnp.int32)
    bins = jnp.arange(freq_total, dtype=jnp.int32)
    window = 0.5 - 0.5 * jnp.cos(2.0 * jnp.pi * times.astype(jnp.float32) / steps_total)
    window_norm = jnp.sqrt(jnp.sum(window * window))
    phases = 2.0 * jnp.pi * (bins[:, None] * times[None, :] % steps_total).astype(jnp.float32) / steps_total
    cos_rows = window[None, :] * jnp.cos(phases) / window_norm
    sin_rows = -window[None, :] * jnp.sin(phases) / window_norm
    return jnp.concatenate([cos_rows, sin_rows], axis=0).astype(jnp.bfloat16)

def select_bins(coefs, freq_ids):
    bin_ids = jnp.arange(coefs.shape[3], dtype=jnp.int32)
    onehot = (freq_ids[:, None] == bin_ids[None, :]).astype(jnp.bfloat16)
    return jnp.einsum('bf,ivcfx->ivcbx', onehot, coefs, preferred_element_type=jnp.float32)

def triad_block(row_coefs, col_coefs, weights, pair_block):
    first_freq = pair_block[:, 0]
    second_freq = pair_block[:, 1]
    sum_freq = first_freq + second_freq
    first_coef = select_bins(row_coefs, first_freq)
    second_coef = select_bins(row_coefs, second_freq)
    partner = select_bins(col_coefs, sum_freq).astype(jnp.bfloat16)
    prod_real = (first_coef[:, :, 0] * second_coef[:, :, 0] - first_coef[:, :, 1] * second_coef[:, :, 1]) * weights
    prod_imag = -(first_coef[:, :, 0] * second_coef[:, :, 1] + first_coef[:, :, 1] * second_coef[:, :, 0]) * weights
    product = jnp.stack([prod_real, prod_imag], axis=2).astype(jnp.bfloat16)
    against_real = jnp.stack([partner[:, :, 0], -partner[:, :, 1]], axis=2)
    against_imag = jnp.stack([partner[:, :, 1], partner[:, :, 0]], axis=2)
    bisp_real = jnp.einsum('rvcbx,jvcbx->brj', product, against_real, preferred_element_type=jnp.float32)
    bisp_imag = jnp.einsum('rvcbx,jvcbx->brj', product, against_imag, preferred_element_type=jnp.float32)
    return jnp.stack([bisp_real, bisp_imag], axis=-1)

def all_triads(row_coefs, col_coefs, weights, triad_pairs, block_size):
    row_split = row_coefs.reshape(row_coefs.shape[0], row_coefs.shape[1], 2, -1, row_coefs.shape[3])
    col_split = col_coefs.reshape(col_coefs.shape[0], col_coefs.shape[1], 2, -1, col_coefs.shape[3])
    pair_blocks = triad_pairs.reshape(-1, block_size, 2)
    result = lax.map(lambda pair_block: triad_block(row_split, col_split, weights, pair_block), pair_blocks)
    return result.reshape((triad_pairs.shape[0],) + result.shape[2:])

def slot_index(owner_counts, triad_total, most_owned):
    ending = jnp.cumsum(owner_counts).astype(jnp.int32)
    starting = ending - owner_counts
    positions = jnp.arange(triad_total, dtype=jnp.int32)
    owner_of = lax.optimization_barrier(jnp.sum((positions[:, None] >= ending[None, :]).astype(jnp.int32), axis=1))
    owner_ids = jnp.arange(owner_counts.shape[0], dtype=jnp.int32)
    start_of = lax.optimization_barrier(jnp.sum(jnp.where(owner_ids[None, :] == owner_of[:, None], starting[None, :], 0), axis=1))
    return (owner_of * most_owned + positions - start_of).astype(jnp.int32)

def reference(snapshots, quad_weights, triad_pairs, owner_counts):
    basis = dft_table(SNAPS, FREQS)
    coeffs = jnp.einsum('fs,ivsx->ivfx', basis.astype(jnp.float32), snapshots.astype(jnp.float32)).astype(jnp.bfloat16)
    weights = quad_weights.astype(jnp.float32)
    weight_total = jnp.sum(weights * weights)
    raw = all_triads(coeffs, coeffs, weights, triad_pairs, 2 * TRI_DEV)
    slot_ids = slot_index(owner_counts, TRIADS, OWN_MOST)
    placed = jnp.zeros((SLOTS,) + raw.shape[1:], jnp.float32).at[slot_ids].set(raw)
    return placed / jnp.sqrt(weight_total)
```

```python
import functools

import jax
import jax.numpy as jnp
import numpy as np
from jax import lax
from jax.experimental import pallas as pl
from jax.experimental.pallas import tpu as pltpu
from jax.sharding import PartitionSpec as P

SNAPS = 256
FREQS = 64
REALS = 8
TRIADS = 512
OWN_MOST = 32
N_REAL = 4
N_CELL = 32
XQ = 512
TB = 32
WIN = 16
ROWS = 9
VMEM = 56 * 1024 * 1024


def dft_table():
    times = np.arange(SNAPS)
    bins = np.arange(FREQS)
    window = 0.5 - 0.5 * np.cos(2.0 * np.pi * times / SNAPS)
    norm = np.sqrt(np.sum(window * window))
    phases = 2.0 * np.pi * ((bins[:, None] * times[None, :]) % SNAPS) / SNAPS
    table = np.concatenate([window * np.cos(phases), -window * np.sin(phases)], axis=0) / norm
    return jnp.asarray(table.astype(np.float32)).astype(jnp.bfloat16)


def dft_kernel(n, where_ref, basis_ref, *refs):
    for s in range(n):
        refs[n + s][0, 0] = jnp.dot(
            basis_ref[...], refs[s][0, 0], preferred_element_type=jnp.float32
        ).astype(jnp.bfloat16)


def dft(where, basis, snapshots, shifts):
    n = len(shifts)

    def source(s):
        return lambda r, v, where: (r, v, 0, lax.rem(where[0] + s, N_REAL))

    return pl.pallas_call(
        functools.partial(dft_kernel, n),
        grid_spec=pltpu.PrefetchScalarGridSpec(
            num_scalar_prefetch=1,
            grid=(2, 2),
            in_specs=[pl.BlockSpec((2 * FREQS, SNAPS), lambda r, v, where: (0, 0))]
            + [pl.BlockSpec((1, 1, SNAPS, XQ), source(s)) for s in shifts],
            out_specs=[pl.BlockSpec((1, 1, 2 * FREQS, XQ), lambda r, v, where: (r, v, 0, 0)) for s in shifts],
        ),
        out_shape=[jax.ShapeDtypeStruct((2, 2, 2 * FREQS, XQ), jnp.bfloat16) for s in shifts],
        compiler_params=pltpu.CompilerParams(vmem_limit_bytes=VMEM),
        cost_estimate=pl.CostEstimate(
            flops=2 * 4 * n * 2 * FREQS * SNAPS * XQ, bytes_accessed=4 * n * 3 * FREQS * 2 * XQ * 2, transcendentals=0
        ),
    )(where, basis, *([snapshots] * n))


def triad_kernel(where_ref, packed_ref, p0, p1, p2, p3, w_ref, out_ref, cf, wc, part, left_a, left_b, full, acc):
    vx = 2 * XQ
    me = where_ref[0]
    for s, piece in enumerate((p0, p1, p2, p3)):
        group = lax.rem(me + N_REAL - s, N_REAL)
        for r in range(2):
            for v in range(2):
                for q in range(XQ // 128):
                    cf[v * (XQ // 128) + q, pl.ds(2 * group + r, 2 * FREQS, stride=REALS), :] = piece[
                        r, v, :, q * 128 : (q + 1) * 128
                    ].astype(jnp.float32)
    tiles = vx // 128
    weights = w_ref[...].astype(jnp.float32)

    def prepare(m, carry):
        re = pl.ds(pl.multiple_of(m * REALS, REALS), REALS)
        im = pl.ds(pl.multiple_of((m + FREQS) * REALS, REALS), REALS)
        rows = pl.ds(pl.multiple_of(m * 2 * REALS, 2 * REALS), 2 * REALS)
        for q in range(tiles):
            at = q % (XQ // 128) * 128
            weight = weights[:, at : at + 128]
            a, b = cf[q, re, :], cf[q, im, :]
            wc[q, re, :] = a * weight
            wc[q, im, :] = b * weight
            part[rows, q * 128 : (q + 1) * 128] = jnp.concatenate([a, b], axis=0).astype(jnp.bfloat16)
            part[rows, vx + q * 128 : vx + (q + 1) * 128] = jnp.concatenate([b, -a], axis=0).astype(jnp.bfloat16)
        return carry

    lax.fori_loop(0, FREQS, prepare, 0, unroll=4)
    acc[...] = jnp.zeros_like(acc)
    lane_group = lax.broadcasted_iota(jnp.int32, (REALS, 128), 1) // (2 * REALS)

    def bins_of(t):
        word = packed_ref[t]
        return word & 63, (word >> 6) & 63, word >> 12

    def build(left, block):
        for pair in range(TB // 2):
            rows = slice(2 * REALS * pair, 2 * REALS * (pair + 1))
            slices = []
            for h in range(2):
                k, l, _ = bins_of(block * TB + 2 * pair + h)
                slices.append([pl.ds(pl.multiple_of(n * REALS, REALS), REALS) for n in (k, k + FREQS, l, l + FREQS)])
            for q in range(tiles):
                reals, imags = [], []
                for kr, ki, lr, li in slices:
                    ak, bk, al, bl = wc[q, kr, :], wc[q, ki, :], cf[q, lr, :], cf[q, li, :]
                    reals.append(ak * al - bk * bl)
                    imags.append(ak * bl + bk * al)
                left[rows, q * 128 : (q + 1) * 128] = jnp.concatenate(reals, axis=0).astype(jnp.bfloat16)
                left[rows, vx + q * 128 : vx + (q + 1) * 128] = jnp.concatenate(imags, axis=0).astype(jnp.bfloat16)

    def window(left, block, first):
        rows = pl.ds(pl.multiple_of(first * 2 * REALS, 2 * REALS), WIN * 2 * REALS)
        prod = lax.dot_general(
            left[...], part[rows, :], (((1,), (1,)), ((), ())), preferred_element_type=jnp.float32
        )
        full[0] = prod[:, :128]
        full[1] = prod[:, 128:]
        for i in range(TB):
            k, l, slot = bins_of(block * TB + i)
            at = k + l - first
            inside = jnp.logical_and(at >= 0, at < WIN)
            at = lax.rem(jnp.maximum(at, 0), WIN)
            tile = full[at // 8, pl.ds(i * REALS, REALS), :]
            turn = lax.rem(lax.rem(slot, 8) - lax.rem(at, 8) + 8, 8) * (2 * REALS)
            tile = pltpu.roll(tile, turn, 1)
            want = jnp.where(inside, lax.rem(slot, 8), -1)
            pltpu.store(
                acc.at[pl.ds(pl.multiple_of((slot // 8) * REALS, REALS), REALS), :], tile, mask=lane_group == want
            )

    def use(left, block):
        k, l, _ = bins_of(block * TB)
        low = k + l
        k, l, _ = bins_of(block * TB + TB - 1)
        high = k + l
        window(left, block, jnp.minimum(low, FREQS - WIN))

        def more(first):
            window(left, block, jnp.minimum(first, FREQS - WIN))
            return first + WIN

        lax.while_loop(lambda first: first <= high, more, low + WIN)

    blocks = TRIADS // TB
    build(left_a, 0)

    def step(i, carry):
        build(left_b, 2 * i + 1)
        use(left_a, 2 * i)
        build(left_a, jnp.minimum(2 * i + 2, blocks - 1))
        use(left_b, 2 * i + 1)
        return carry

    lax.fori_loop(0, blocks // 2, step, 0)

    own = w_ref[...].astype(jnp.float32)
    square = jnp.sum(own * own, axis=1, keepdims=True)
    square = jnp.broadcast_to(square, (1, 128))
    for o in range(N_CELL):
        for y in range(N_REAL):
            to = ROWS * (o * N_REAL + y)
            for r in range(2):
                out_ref[to + 4 * r : to + 4 * r + 4, :] = acc[pl.ds(o * 32 + 2 * y + r, 4, stride=REALS), :]
            out_ref[to + 8 : to + 9, :] = square


def triads(where, packed, pieces, quad_weights):
    vx = 2 * XQ
    whole = pl.BlockSpec((2, 2, 2 * FREQS, XQ), lambda i, where, packed: (0, 0, 0, 0))
    return pl.pallas_call(
        triad_kernel,
        grid_spec=pltpu.PrefetchScalarGridSpec(
            num_scalar_prefetch=2,
            grid=(1,),
            in_specs=[whole] * 4 + [pl.BlockSpec((1, XQ), lambda i, where, packed: (0, where[0]))],
            out_specs=pl.BlockSpec((N_CELL * N_REAL * ROWS, 128), lambda i, where, packed: (0, 0)),
            scratch_shapes=[
                pltpu.VMEM((vx // 128, 2 * FREQS * REALS, 128), jnp.float32),
                pltpu.VMEM((vx // 128, 2 * FREQS * REALS, 128), jnp.float32),
                pltpu.VMEM((2 * FREQS * REALS, 2 * vx), jnp.bfloat16),
                pltpu.VMEM((TB * REALS, 2 * vx), jnp.bfloat16),
                pltpu.VMEM((TB * REALS, 2 * vx), jnp.bfloat16),
                pltpu.VMEM((2, TB * REALS, 128), jnp.float32),
                pltpu.VMEM((N_CELL * OWN_MOST, 128), jnp.float32),
            ],
        ),
        out_shape=jax.ShapeDtypeStruct((N_CELL * N_REAL * ROWS, 128), jnp.float32),
        compiler_params=pltpu.CompilerParams(vmem_limit_bytes=VMEM),
        cost_estimate=pl.CostEstimate(flops=10_000_000_000, bytes_accessed=4 * 1024 * 1024, transcendentals=0),
    )(where, packed, *pieces, quad_weights)


def sorted_words(triad_pairs, owner_counts):
    ids = jnp.arange(TRIADS, dtype=jnp.int32)
    owners = jnp.arange(N_CELL, dtype=jnp.int32)
    ending = jnp.sum(jnp.where(owners[None, :] <= owners[:, None], owner_counts[None, :], 0), axis=1)
    past = ids[:, None] >= ending[None, :]
    owner = jnp.sum(past.astype(jnp.int32), axis=1)
    start = jnp.sum(jnp.where(past, owner_counts[None, :], 0), axis=1)
    slot = owner * OWN_MOST + ids - start
    first, second = triad_pairs[:, 0], triad_pairs[:, 1]
    key = (first + second) * TRIADS + ids
    rank = jnp.sum((key[None, :] < key[:, None]).astype(jnp.int32), axis=1)
    word = first + second * FREQS + slot * FREQS * FREQS
    return jnp.sum(jnp.where(rank[None, :] == ids[:, None], word[None, :], 0), axis=1)


def local(snapshots, quad_weights, triad_pairs, owner_counts):
    basis = dft_table()
    where = lax.axis_index("real").astype(jnp.int32).reshape(1)
    away = dft(where, basis, snapshots, (2, 1, 3))
    arrived = [
        lax.ppermute(piece, "real", [(i, (i + s) % N_REAL) for i in range(N_REAL)])
        for piece, s in zip(away, (2, 1, 3))
    ]
    (own,) = dft(where, basis, snapshots, (0,))
    words = sorted_words(triad_pairs, owner_counts)
    sums = triads(where, words, (own, arrived[1], arrived[0], arrived[2]), quad_weights.reshape(1, -1))
    sums = sums.reshape(N_CELL * N_REAL, 1, ROWS * 128)
    received = lax.all_to_all(sums, ("cell", "real"), split_axis=0, concat_axis=0, tiled=True)
    total = jnp.sum(received, axis=(0, 1))
    values = total[: 8 * 128].reshape(2, 4, 8, 2, REALS)
    values = jnp.transpose(values, (1, 2, 0, 4, 3)).reshape(OWN_MOST, 2, REALS, 2)
    return values / jnp.sqrt(total[8 * 128])


def solution(mesh):
    return jax.shard_map(
        local,
        mesh=mesh,
        in_specs=(P("real", None, None, "cell"), P("cell"), P(), P()),
        out_specs=P("cell", "real", None, None),
        check_vma=False,
    )
```

```python
import functools

import jax
import jax.numpy as jnp
import numpy as np
from jax import lax
from jax.experimental import pallas as pl
from jax.experimental.pallas import tpu as pltpu
from jax.sharding import PartitionSpec as P

SNAPS = 256
FREQS = 64
REALS = 8
TRIADS = 512
OWN_MOST = 32
N_REAL = 4
N_CELL = 32
XQ = 512
PARTS = ((0, 256), (256, 256))
TB = 64
WIN = 16
WIN_FIRST = 32
ROWS = 9
VMEM_SPACE = pl.BlockSpec(memory_space=pltpu.VMEM)
SMEM_SPACE = pl.BlockSpec(memory_space=pltpu.SMEM)


def dft_table():
    times = np.arange(SNAPS)
    bins = np.arange(FREQS)
    window = 0.5 - 0.5 * np.cos(2.0 * np.pi * times / SNAPS)
    norm = np.sqrt(np.sum(window * window))
    phases = 2.0 * np.pi * ((bins[:, None] * times[None, :]) % SNAPS) / SNAPS
    table = np.concatenate([window * np.cos(phases), -window * np.sin(phases)], axis=0) / norm
    return jnp.asarray(table.astype(np.float32)).astype(jnp.bfloat16)


def dft_kernel(jobs, where_ref, basis_ref, snapshots_ref, *refs):
    n = len(jobs)
    outs, bufs, sems = refs[:n], refs[n : 2 * n], refs[2 * n]
    copies = []
    for i, (s, start, width) in enumerate(jobs):
        at = pl.multiple_of(lax.rem(where_ref[0] + s, N_REAL) * XQ + start, 128)
        copies.append(
            pltpu.make_async_copy(snapshots_ref.at[:, :, :, pl.ds(at, width)], bufs[i], sems.at[i])
        )
        copies[-1].start()
    for i in range(n):
        copies[i].wait()
        for r in range(2):
            for v in range(2):
                outs[i][r, v] = jnp.dot(
                    basis_ref[...], bufs[i][r, v], preferred_element_type=jnp.float32
                ).astype(jnp.bfloat16)


def dft(where, basis, snapshots, jobs):
    n, cells = len(jobs), sum(width for _, _, width in jobs)
    return pl.pallas_call(
        functools.partial(dft_kernel, jobs),
        in_specs=[SMEM_SPACE, VMEM_SPACE, pl.BlockSpec(memory_space=pltpu.HBM)],
        out_specs=[VMEM_SPACE] * n,
        out_shape=[jax.ShapeDtypeStruct((2, 2, 2 * FREQS, width), jnp.bfloat16) for _, _, width in jobs],
        scratch_shapes=[pltpu.VMEM((2, 2, SNAPS, width), jnp.bfloat16) for _, _, width in jobs]
        + [pltpu.SemaphoreType.DMA((n,))],
        compiler_params=pltpu.CompilerParams(vmem_limit_bytes=16 * 1024 * 1024),
        cost_estimate=pl.CostEstimate(
            flops=2 * 4 * 2 * FREQS * SNAPS * cells, bytes_accessed=4 * SNAPS * 2 * cells, transcendentals=0
        ),
    )(where, basis, snapshots)


def triad_kernel(start, width, last, where_ref, pairs_ref, places_ref, spans_ref, p0, p1, p2, p3, w_ref, *refs):
    if last:
        before, out_ref, cf, part, left_a, left_b, full_a, full_b, acc = refs
    else:
        acc, cf, part, left_a, left_b, full_a, full_b = refs
    vx = 2 * width
    tiles = vx // 128
    me = where_ref[0]
    for s, piece in enumerate((p0, p1, p2, p3)):
        group = lax.rem(me + N_REAL - s, N_REAL)
        for r in range(2):
            for v in range(2):
                for q in range(width // 128):
                    cf[v * (width // 128) + q, pl.ds(2 * group + r, 2 * FREQS, stride=REALS), :] = piece[
                        r, v, :, q * 128 : (q + 1) * 128
                    ].astype(jnp.float32)
    weights = [
        w_ref[:, pl.ds(pl.multiple_of(me * XQ + start + q * 128, 128), 128)].astype(jnp.float32)
        for q in range(width // 128)
    ]
    weights = [jnp.broadcast_to(weight, (REALS, 128)) for weight in weights]

    def prepare(m, carry):
        re = pl.ds(pl.multiple_of(m * REALS, REALS), REALS)
        im = pl.ds(pl.multiple_of((m + FREQS) * REALS, REALS), REALS)
        rows = pl.ds(pl.multiple_of(m * 2 * REALS, 2 * REALS), 2 * REALS)
        for q in range(tiles):
            a, b = cf[q, re, :], cf[q, im, :]
            part[rows, q * 128 : (q + 1) * 128] = jnp.concatenate([a, b], axis=0).astype(jnp.bfloat16)
            part[rows, vx + q * 128 : vx + (q + 1) * 128] = jnp.concatenate([b, -a], axis=0).astype(jnp.bfloat16)
        return carry

    lax.fori_loop(0, FREQS, prepare, 0, unroll=4)
    acc[...] = jnp.zeros_like(acc)
    lane_group = lax.broadcasted_iota(jnp.int32, (REALS, 128), 1) // (2 * REALS)

    def build(left, block):
        for pair in range(TB // 2):
            rows = slice(2 * REALS * pair, 2 * REALS * (pair + 1))
            slices = []
            for h in range(2):
                word = pairs_ref[block * TB + 2 * pair + h]
                slices.append([pl.ds(pl.multiple_of(n, 2 * REALS), 2 * REALS) for n in (word & 1023, word >> 10)])
            for q in range(tiles):
                lanes = slice(q * 128, (q + 1) * 128)
                weight = weights[q % (width // 128)]
                reals, imags = [], []
                for kr, lr in slices:
                    k, l = part[kr, lanes].astype(jnp.float32), part[lr, lanes].astype(jnp.float32)
                    ak, bk, al, bl = k[:REALS], k[REALS:], l[:REALS], l[REALS:]
                    reals.append((ak * al - bk * bl) * weight)
                    imags.append((ak * bl + bk * al) * weight)
                left[rows, lanes] = jnp.concatenate(reals, axis=0).astype(jnp.bfloat16)
                left[rows, vx + q * 128 : vx + (q + 1) * 128] = jnp.concatenate(imags, axis=0).astype(jnp.bfloat16)

    def multiply(left, full, first, win=WIN):
        rows = pl.ds(pl.multiple_of(first * 2 * REALS, 2 * REALS), win * 2 * REALS)
        prod = lax.dot_general(
            left[...], part[rows, :], (((1,), (1,)), ((), ())), preferred_element_type=jnp.float32
        )
        for c in range(win // 8):
            full[c] = prod[:, c * 128 : (c + 1) * 128]

    def put(full, i, row, half, turn, want):
        tile = pltpu.roll(full[half, pl.ds(i * REALS, REALS), :], turn, 1)
        pltpu.store(acc.at[pl.ds(pl.multiple_of(row, REALS), REALS), :], tile, mask=lane_group == want)

    def extract(full, block):
        for i in range(TB):
            word = places_ref[block * TB + i]
            put(full, i, word & 1016, (word >> 10) & 3, (word >> 8) & 112, word >> 15)

    blocks = TRIADS // TB
    build(left_a, 0)
    multiply(left_a, full_a, spans_ref[0], WIN_FIRST)
    build(left_b, 1)

    def stage(left, full, block, left_next, full_last):
        multiply(left, full, spans_ref[block])
        build(left_next, jnp.minimum(block + 1, blocks - 1))
        extract(full_last, block - 1)

    def step(i, carry):
        stage(left_b, full_b, 2 * i + 1, left_a, full_a)
        stage(left_a, full_a, 2 * i + 2, left_b, full_b)
        return carry

    lax.fori_loop(0, blocks // 2 - 1, step, 0)
    stage(left_b, full_b, blocks - 1, left_a, full_a)
    extract(full_b, blocks - 1)

    def beyond(block, carry):
        high = spans_ref[blocks + block]

        def more(first):
            low = jnp.minimum(first, FREQS - WIN)
            build(left_a, block)
            multiply(left_a, full_a, low)

            def one(i, carry):
                pair, slot = pairs_ref[block * TB + i], places_ref[block * TB + i] & 1023
                at = ((pair & 1023) + (pair >> 10)) // (2 * REALS) - low
                inside = jnp.logical_and(at >= 0, at < WIN)
                at = at & (WIN - 1)
                turn = ((slot - at) & 7) * (2 * REALS)
                put(full_a, i, slot & 1016, at >> 3, turn, jnp.where(inside, slot & 7, -1))
                return carry

            lax.fori_loop(0, TB, one, 0)
            return first + WIN

        lax.while_loop(lambda first: first <= high, more, spans_ref[block] + jnp.where(block == 0, WIN_FIRST, WIN))
        return carry

    lax.fori_loop(0, blocks, beyond, 0)

    if last:
        own = w_ref[:, pl.ds(pl.multiple_of(me * XQ, 128), XQ)].astype(jnp.float32)
        square = jnp.broadcast_to(jnp.sum(own * own, axis=1, keepdims=True), (1, 128))
        for o in range(N_CELL):
            for y in range(N_REAL):
                to = ROWS * (o * N_REAL + y)
                for r in range(2):
                    rows = pl.ds(o * OWN_MOST + 2 * y + r, 4, stride=REALS)
                    out_ref[to + 4 * r : to + 4 * r + 4, :] = acc[rows, :] + before[rows, :]
                out_ref[to + 8 : to + 9, :] = square


def triads(where, plan, pieces, quad_weights, start, width, before=None):
    vx, last = 2 * width, before is not None
    sums = jax.ShapeDtypeStruct((N_CELL * OWN_MOST, 128), jnp.float32)
    sent = jax.ShapeDtypeStruct((N_CELL * N_REAL * ROWS, 128), jnp.float32)
    return pl.pallas_call(
        functools.partial(triad_kernel, start, width, last),
        in_specs=[SMEM_SPACE] * 4 + [VMEM_SPACE] * (6 if last else 5),
        out_specs=VMEM_SPACE,
        scratch_shapes=[
            pltpu.VMEM((vx // 128, 2 * FREQS * REALS, 128), jnp.float32),
            pltpu.VMEM((2 * FREQS * REALS, 2 * vx), jnp.bfloat16),
            pltpu.VMEM((TB * REALS, 2 * vx), jnp.bfloat16),
            pltpu.VMEM((TB * REALS, 2 * vx), jnp.bfloat16),
            pltpu.VMEM((WIN_FIRST // 8, TB * REALS, 128), jnp.float32),
            pltpu.VMEM((WIN_FIRST // 8, TB * REALS, 128), jnp.float32),
        ]
        + ([pltpu.VMEM(sums.shape, jnp.float32)] if last else []),
        out_shape=sent if last else sums,
        compiler_params=pltpu.CompilerParams(vmem_limit_bytes=24 * 1024 * 1024),
        cost_estimate=pl.CostEstimate(flops=20_000_000 * width, bytes_accessed=2 * 1024 * 1024, transcendentals=0),
    )(where, *plan, *pieces, quad_weights, *([before] if last else []))


def triad_plan(triad_pairs, owner_counts):
    ids = jnp.arange(TRIADS, dtype=jnp.int32)
    owners = jnp.arange(N_CELL, dtype=jnp.int32)
    ending = jnp.sum(jnp.where(owners[None, :] <= owners[:, None], owner_counts[None, :], 0), axis=1)
    past = ids[:, None] >= ending[None, :]
    owner = jnp.sum(past.astype(jnp.int32), axis=1)
    start = jnp.sum(jnp.where(past, owner_counts[None, :], 0), axis=1)
    slot = owner * OWN_MOST + ids - start
    first, second = triad_pairs[:, 0], triad_pairs[:, 1]
    key = (first + second) * TRIADS + ids
    rank = jnp.sum((key[None, :] < key[:, None]).astype(jnp.int32), axis=1)
    word = first + second * FREQS + slot * FREQS * FREQS
    word = jnp.sum(jnp.where(rank[None, :] == ids[:, None], word[None, :], 0), axis=1)
    first, second, slot = word & 63, (word >> 6) & 63, word >> 12
    total = (first + second).reshape(-1, TB)
    win = jnp.where(jnp.arange(TRIADS // TB) == 0, WIN_FIRST, WIN)
    low, high = jnp.minimum(total[:, 0], FREQS - win), total[:, TB - 1]
    at = (total - low[:, None]).reshape(-1)
    outside = ((total - low[:, None]) >= win[:, None]).reshape(-1).astype(jnp.int32)
    turn = (slot - at) & 7
    places = slot + (((at >> 3) & 3) << 10) + (turn << 12) + (((slot & 7) + 8 * outside) << 15)
    pairs = first * 2 * REALS + ((second * 2 * REALS) << 10)
    return pairs, places, jnp.concatenate([low, high])


def local(snapshots, quad_weights, triad_pairs, owner_counts):
    basis = dft_table()
    where = lax.axis_index("real").astype(jnp.int32).reshape(1)
    weights = quad_weights.reshape(1, -1)
    plan = triad_plan(triad_pairs, owner_counts)
    shifts = (2, 1, 3)
    arrived = []
    for start, width in PARTS:
        away = dft(where, basis, snapshots, tuple((s, start, width) for s in shifts))
        moved = [
            lax.ppermute(piece, "real", [(i, (i + s) % N_REAL) for i in range(N_REAL)])
            for piece, s in zip(away, shifts)
        ]
        arrived.append((moved[1], moved[0], moved[2]))
    own = dft(where, basis, snapshots, tuple((0, start, width) for start, width in PARTS))
    sums = None
    for (start, width), pieces, here in zip(PARTS, arrived, own):
        sums = triads(where, plan, (here,) + pieces, weights, start, width, sums)
    sums = sums.reshape(N_CELL * N_REAL, 1, ROWS * 128)
    received = lax.all_to_all(sums, ("cell", "real"), split_axis=0, concat_axis=0, tiled=True)
    total = jnp.sum(received, axis=(0, 1))
    values = total[: 8 * 128].reshape(2, 4, 8, 2, REALS)
    values = jnp.transpose(values, (1, 2, 0, 4, 3)).reshape(OWN_MOST, 2, REALS, 2)
    return values / jnp.sqrt(total[8 * 128])


def solution(mesh):
    return jax.shard_map(
        local,
        mesh=mesh,
        in_specs=(P("real", None, None, "cell"), P("cell"), P(), P()),
        out_specs=P("cell", "real", None, None),
        check_vma=False,
    )
```

```python
import functools

import jax
import jax.numpy as jnp
import numpy as np
from jax import lax
from jax.experimental import pallas as pl
from jax.experimental.pallas import tpu as pltpu
from jax.sharding import PartitionSpec as P

SNAPS = 256
FREQS = 64
REALS = 8
TRIADS = 512
OWN_MOST = 32
N_REAL = 4
N_CELL = 32
XQ = 512
PARTS = ((0, 256), (256, 256))
TB = 64
WIN = 16
WIN_FIRST = 32
ROWS = 9
DFT_VMEM = 115 * 512 * 1024
VMEM_SPACE = pl.BlockSpec(memory_space=pltpu.VMEM)
SMEM_SPACE = pl.BlockSpec(memory_space=pltpu.SMEM)


def dft_table():
    times = np.arange(SNAPS)
    bins = np.arange(FREQS)
    window = 0.5 - 0.5 * np.cos(2.0 * np.pi * times / SNAPS)
    norm = np.sqrt(np.sum(window * window))
    phases = 2.0 * np.pi * ((bins[:, None] * times[None, :]) % SNAPS) / SNAPS
    table = np.concatenate([window * np.cos(phases), -window * np.sin(phases)], axis=0) / norm
    return jnp.asarray(table.astype(np.float32)).astype(jnp.bfloat16)


def dft_kernel(jobs, after, where_ref, basis_ref, snapshots_ref, *refs):
    n, refs = len(jobs), refs[after:]
    outs, bufs, basis, sems = refs[:n], refs[n : 2 * n], refs[2 * n], refs[2 * n + 1]
    table = pltpu.make_async_copy(basis_ref, basis, sems.at[n])
    table.start()
    copies = []
    for i, (s, start, width) in enumerate(jobs):
        at = pl.multiple_of(lax.rem(where_ref[0] + s, N_REAL) * XQ + start, 128)
        copies.append(
            pltpu.make_async_copy(snapshots_ref.at[:, :, :, pl.ds(at, width)], bufs[i], sems.at[i])
        )
        copies[-1].start()
    table.wait()
    for i in range(n):
        copies[i].wait()
        for r in range(2):
            for v in range(2):
                outs[i][r, v] = jnp.dot(
                    basis[...], bufs[i][r, v], preferred_element_type=jnp.float32
                ).astype(jnp.bfloat16)


def dft(where, basis, snapshots, jobs, after=()):
    n, cells = len(jobs), sum(width for _, _, width in jobs)
    return pl.pallas_call(
        functools.partial(dft_kernel, jobs, len(after)),
        in_specs=[SMEM_SPACE] + [pl.BlockSpec(memory_space=pl.ANY)] * (2 + len(after)),
        out_specs=[VMEM_SPACE] * n,
        out_shape=[jax.ShapeDtypeStruct((2, 2, 2 * FREQS, width), jnp.bfloat16) for _, _, width in jobs],
        scratch_shapes=[pltpu.VMEM((2, 2, SNAPS, width), jnp.bfloat16) for _, _, width in jobs]
        + [pltpu.VMEM((2 * FREQS, SNAPS), jnp.bfloat16), pltpu.SemaphoreType.DMA((n + 1,))],
        compiler_params=pltpu.CompilerParams(vmem_limit_bytes=DFT_VMEM),
        cost_estimate=pl.CostEstimate(
            flops=2 * 4 * 2 * FREQS * SNAPS * cells, bytes_accessed=4 * SNAPS * 2 * cells, transcendentals=0
        ),
    )(where, basis, snapshots, *after)


def triad_kernel(start, width, last, where_ref, pairs_ref, places_ref, spans_ref, p0, p1, p2, p3, w_ref, *refs):
    if last:
        before, out_ref, cf, part, left_a, left_b, full_a, full_b, acc = refs
    else:
        acc, cf, part, left_a, left_b, full_a, full_b = refs
    vx = 2 * width
    tiles = vx // 128
    me = where_ref[0]
    for s, piece in enumerate((p0, p1, p2, p3)):
        group = lax.rem(me + N_REAL - s, N_REAL)
        for r in range(2):
            for v in range(2):
                for q in range(width // 128):
                    cf[v * (width // 128) + q, pl.ds(2 * group + r, 2 * FREQS, stride=REALS), :] = piece[
                        r, v, :, q * 128 : (q + 1) * 128
                    ].astype(jnp.float32)
    weights = [
        w_ref[:, pl.ds(pl.multiple_of(me * XQ + start + q * 128, 128), 128)].astype(jnp.float32)
        for q in range(width // 128)
    ]
    weights = [jnp.broadcast_to(weight, (REALS, 128)) for weight in weights]

    def prepare(m, carry):
        re = pl.ds(pl.multiple_of(m * REALS, REALS), REALS)
        im = pl.ds(pl.multiple_of((m + FREQS) * REALS, REALS), REALS)
        rows = pl.ds(pl.multiple_of(m * 2 * REALS, 2 * REALS), 2 * REALS)
        for q in range(tiles):
            a, b = cf[q, re, :], cf[q, im, :]
            part[rows, q * 128 : (q + 1) * 128] = jnp.concatenate([a, b], axis=0).astype(jnp.bfloat16)
            part[rows, vx + q * 128 : vx + (q + 1) * 128] = jnp.concatenate([b, -a], axis=0).astype(jnp.bfloat16)
        return carry

    lax.fori_loop(0, FREQS, prepare, 0, unroll=4)
    acc[...] = jnp.zeros_like(acc)
    lane_group = lax.broadcasted_iota(jnp.int32, (REALS, 128), 1) // (2 * REALS)

    def build(left, block):
        for pair in range(TB // 2):
            rows = slice(2 * REALS * pair, 2 * REALS * (pair + 1))
            slices = []
            for h in range(2):
                word = pairs_ref[block * TB + 2 * pair + h]
                slices.append([pl.ds(pl.multiple_of(n, 2 * REALS), 2 * REALS) for n in (word & 1023, word >> 10)])
            for q in range(tiles):
                lanes = slice(q * 128, (q + 1) * 128)
                weight = weights[q % (width // 128)]
                reals, imags = [], []
                for kr, lr in slices:
                    k, l = part[kr, lanes].astype(jnp.float32), part[lr, lanes].astype(jnp.float32)
                    ak, bk, al, bl = k[:REALS], k[REALS:], l[:REALS], l[REALS:]
                    reals.append((ak * al - bk * bl) * weight)
                    imags.append((ak * bl + bk * al) * weight)
                left[rows, lanes] = jnp.concatenate(reals, axis=0).astype(jnp.bfloat16)
                left[rows, vx + q * 128 : vx + (q + 1) * 128] = jnp.concatenate(imags, axis=0).astype(jnp.bfloat16)

    def multiply(left, full, first, win=WIN):
        rows = pl.ds(pl.multiple_of(first * 2 * REALS, 2 * REALS), win * 2 * REALS)
        prod = lax.dot_general(
            left[...], part[rows, :], (((1,), (1,)), ((), ())), preferred_element_type=jnp.float32
        )
        for c in range(win // 8):
            full[c] = prod[:, c * 128 : (c + 1) * 128]

    def put(full, i, row, half, turn, want):
        tile = pltpu.roll(full[half, pl.ds(i * REALS, REALS), :], turn, 1)
        pltpu.store(acc.at[pl.ds(pl.multiple_of(row, REALS), REALS), :], tile, mask=lane_group == want)

    def extract(full, block):
        for i in range(TB):
            word = places_ref[block * TB + i]
            put(full, i, word & 1016, (word >> 10) & 3, (word >> 8) & 112, word >> 15)

    blocks = TRIADS // TB
    build(left_a, 0)
    multiply(left_a, full_a, spans_ref[0], WIN_FIRST)
    build(left_b, 1)

    def stage(left, full, block, left_next, full_last):
        multiply(left, full, spans_ref[block])
        build(left_next, jnp.minimum(block + 1, blocks - 1))
        extract(full_last, block - 1)

    def step(i, carry):
        stage(left_b, full_b, 2 * i + 1, left_a, full_a)
        stage(left_a, full_a, 2 * i + 2, left_b, full_b)
        return carry

    lax.fori_loop(0, blocks // 2 - 1, step, 0)
    stage(left_b, full_b, blocks - 1, left_a, full_a)
    extract(full_b, blocks - 1)

    def beyond(block, carry):
        high = spans_ref[blocks + block]

        def more(first):
            low = jnp.minimum(first, FREQS - WIN)
            build(left_a, block)
            multiply(left_a, full_a, low)

            def one(i, carry):
                pair, slot = pairs_ref[block * TB + i], places_ref[block * TB + i] & 1023
                at = ((pair & 1023) + (pair >> 10)) // (2 * REALS) - low
                inside = jnp.logical_and(at >= 0, at < WIN)
                at = at & (WIN - 1)
                turn = ((slot - at) & 7) * (2 * REALS)
                put(full_a, i, slot & 1016, at >> 3, turn, jnp.where(inside, slot & 7, -1))
                return carry

            lax.fori_loop(0, TB, one, 0)
            return first + WIN

        lax.while_loop(lambda first: first <= high, more, spans_ref[block] + jnp.where(block == 0, WIN_FIRST, WIN))
        return carry

    lax.fori_loop(0, blocks, beyond, 0)

    if last:
        own = w_ref[:, pl.ds(pl.multiple_of(me * XQ, 128), XQ)].astype(jnp.float32)
        square = jnp.broadcast_to(jnp.sum(own * own, axis=1, keepdims=True), (1, 128))
        for o in range(N_CELL):
            for y in range(N_REAL):
                to = ROWS * (o * N_REAL + y)
                for r in range(2):
                    rows = pl.ds(o * OWN_MOST + 2 * y + r, 4, stride=REALS)
                    out_ref[to + 4 * r : to + 4 * r + 4, :] = acc[rows, :] + before[rows, :]
                out_ref[to + 8 : to + 9, :] = square


def triads(where, plan, pieces, quad_weights, start, width, before=None):
    vx, last = 2 * width, before is not None
    sums = jax.ShapeDtypeStruct((N_CELL * OWN_MOST, 128), jnp.float32)
    sent = jax.ShapeDtypeStruct((N_CELL * N_REAL * ROWS, 128), jnp.float32)
    return pl.pallas_call(
        functools.partial(triad_kernel, start, width, last),
        in_specs=[SMEM_SPACE] * 4 + [VMEM_SPACE] * (6 if last else 5),
        out_specs=VMEM_SPACE,
        scratch_shapes=[
            pltpu.VMEM((vx // 128, 2 * FREQS * REALS, 128), jnp.float32),
            pltpu.VMEM((2 * FREQS * REALS, 2 * vx), jnp.bfloat16),
            pltpu.VMEM((TB * REALS, 2 * vx), jnp.bfloat16),
            pltpu.VMEM((TB * REALS, 2 * vx), jnp.bfloat16),
            pltpu.VMEM((WIN_FIRST // 8, TB * REALS, 128), jnp.float32),
            pltpu.VMEM((WIN_FIRST // 8, TB * REALS, 128), jnp.float32),
        ]
        + ([pltpu.VMEM(sums.shape, jnp.float32)] if last else []),
        out_shape=sent if last else sums,
        compiler_params=pltpu.CompilerParams(vmem_limit_bytes=24 * 1024 * 1024),
        cost_estimate=pl.CostEstimate(flops=20_000_000 * width, bytes_accessed=2 * 1024 * 1024, transcendentals=0),
    )(where, *plan, *pieces, quad_weights, *([before] if last else []))


def finish_kernel(received_ref, out_ref, sums):
    period = 8 * ROWS
    total = received_ref[0:period, :]
    for i in range(1, N_CELL * N_REAL * ROWS // period):
        total = total + received_ref[i * period : (i + 1) * period, :]
    sums[...] = total
    rows = [jnp.sum(sums[pl.ds(r, 8, stride=ROWS), :], axis=0, keepdims=True) for r in range(ROWS)]
    scale = 1.0 / jnp.sqrt(rows[8])
    values = jnp.concatenate([row * scale for row in rows[:8]], axis=0)
    turned = jnp.concatenate([values, jnp.zeros((120, 128), jnp.float32)], axis=0).T
    lane = lax.broadcasted_iota(jnp.int32, (2 * REALS, 128), 1)
    for i in range(2):
        placed = jnp.zeros((2 * REALS, 128), jnp.float32)
        for t in range(8):
            piece = turned[t * 2 * REALS : (t + 1) * 2 * REALS, :]
            placed = jnp.where(lane // 4 == t, pltpu.roll(piece, (4 * t - 4 * i) % 128, 1), placed)
        for c in range(2):
            for j in range(REALS):
                out_ref[i, j, c : c + 1, :] = placed[c * REALS + j : c * REALS + j + 1, :OWN_MOST]


def finish(received):
    return pl.pallas_call(
        finish_kernel,
        in_specs=[VMEM_SPACE],
        out_specs=VMEM_SPACE,
        scratch_shapes=[pltpu.VMEM((8 * ROWS, 128), jnp.float32)],
        out_shape=jax.ShapeDtypeStruct((2, REALS, 2, OWN_MOST), jnp.float32),
        compiler_params=pltpu.CompilerParams(vmem_limit_bytes=4 * 1024 * 1024),
    )(received)


def triad_plan(triad_pairs, owner_counts):
    ids = jnp.arange(TRIADS, dtype=jnp.int32)
    owners = jnp.arange(N_CELL, dtype=jnp.int32)
    ending = jnp.sum(jnp.where(owners[None, :] <= owners[:, None], owner_counts[None, :], 0), axis=1)
    past = ids[:, None] >= ending[None, :]
    owner = jnp.sum(past.astype(jnp.int32), axis=1)
    start = jnp.sum(jnp.where(past, owner_counts[None, :], 0), axis=1)
    place = ids - start
    slot = owner * OWN_MOST + (place & 3) * 8 + (place >> 2)
    first, second = triad_pairs[:, 0], triad_pairs[:, 1]
    key = (first + second) * TRIADS + ids
    rank = jnp.sum((key[None, :] < key[:, None]).astype(jnp.int32), axis=1)
    word = first + second * FREQS + slot * FREQS * FREQS
    word = jnp.sum(jnp.where(rank[None, :] == ids[:, None], word[None, :], 0), axis=1)
    first, second, slot = word & 63, (word >> 6) & 63, word >> 12
    total = (first + second).reshape(-1, TB)
    win = jnp.where(jnp.arange(TRIADS // TB) == 0, WIN_FIRST, WIN)
    low, high = jnp.minimum(total[:, 0], FREQS - win), total[:, TB - 1]
    at = (total - low[:, None]).reshape(-1)
    outside = ((total - low[:, None]) >= win[:, None]).reshape(-1).astype(jnp.int32)
    turn = (slot - at) & 7
    places = slot + (((at >> 3) & 3) << 10) + (turn << 12) + (((slot & 7) + 8 * outside) << 15)
    pairs = first * 2 * REALS + ((second * 2 * REALS) << 10)
    return pairs, places, jnp.concatenate([low, high])


def local(snapshots, quad_weights, triad_pairs, owner_counts):
    basis = dft_table()
    where = lax.axis_index("real").astype(jnp.int32).reshape(1)
    weights = quad_weights.reshape(1, -1)
    plan = triad_plan(triad_pairs, owner_counts)
    shifts = (1, 3, 2)
    (first, width), (second, width2) = PARTS
    early = tuple((s, first, width) for s in shifts) + ((0, first, width), (0, second, width2))
    early = dft(where, basis, snapshots, early)
    late = dft(where, basis, snapshots, tuple((s, second, width2) for s in shifts), (early[0],))
    away, own = [early[:3], late], early[3:]
    arrived = []
    for pieces in away:
        moved = [
            lax.ppermute(piece, "real", [(i, (i + s) % N_REAL) for i in range(N_REAL)])
            for piece, s in zip(pieces, shifts)
        ]
        arrived.append((moved[0], moved[2], moved[1]))
    sums = None
    for (start, width), pieces, here in zip(PARTS, arrived, own):
        sums = triads(where, plan, (here,) + pieces, weights, start, width, sums)
    sums = sums.reshape(N_CELL * N_REAL, 1, ROWS * 128)
    received = lax.all_to_all(sums, ("cell", "real"), split_axis=0, concat_axis=0, tiled=True)
    values = finish(received.reshape(N_CELL * N_REAL * ROWS, 128))
    return jnp.transpose(values, (3, 0, 1, 2))


def solution(mesh):
    return jax.shard_map(
        local,
        mesh=mesh,
        in_specs=(P("real", None, None, "cell"), P("cell"), P(), P()),
        out_specs=P("cell", "real", None, None),
        check_vma=False,
    )
```

```python
import functools

import jax
import jax.numpy as jnp
import numpy as np
from jax import lax
from jax.experimental import pallas as pl
from jax.experimental.pallas import tpu as pltpu
from jax.sharding import PartitionSpec as P

SNAPS = 256
FREQS = 64
REALS = 8
TRIADS = 512
OWN_MOST = 32
N_REAL = 4
N_CELL = 32
XQ = 512
PARTS = ((0, 256), (256, 256))
TB = 64
WIN = 16
WIN_FIRST = 32
ROWS = 9
DFT_VMEM = 115 * 512 * 1024
VMEM_SPACE = pl.BlockSpec(memory_space=pltpu.VMEM)
SMEM_SPACE = pl.BlockSpec(memory_space=pltpu.SMEM)


def dft_table():
    times = np.arange(SNAPS)
    bins = np.arange(FREQS)
    window = 0.5 - 0.5 * np.cos(2.0 * np.pi * times / SNAPS)
    norm = np.sqrt(np.sum(window * window))
    phases = 2.0 * np.pi * ((bins[:, None] * times[None, :]) % SNAPS) / SNAPS
    table = np.concatenate([window * np.cos(phases), -window * np.sin(phases)], axis=0) / norm
    return jnp.asarray(table.astype(np.float32)).astype(jnp.bfloat16)


def dft_kernel(jobs, after, where_ref, basis_ref, snapshots_ref, *refs):
    n, refs = len(jobs), refs[after:]
    outs, bufs, basis, sems = refs[:n], refs[n : 2 * n], refs[2 * n], refs[2 * n + 1]
    table = pltpu.make_async_copy(basis_ref, basis, sems.at[n])
    table.start()
    copies = []
    for i, (s, start, width) in enumerate(jobs):
        at = pl.multiple_of(lax.rem(where_ref[0] + s, N_REAL) * XQ + start, 128)
        copies.append(
            pltpu.make_async_copy(snapshots_ref.at[:, :, :, pl.ds(at, width)], bufs[i], sems.at[i])
        )
        copies[-1].start()
    table.wait()
    for i in range(n):
        copies[i].wait()
        for r in range(2):
            for v in range(2):
                outs[i][r, v] = jnp.dot(
                    basis[...], bufs[i][r, v], preferred_element_type=jnp.float32
                ).astype(jnp.bfloat16)


def dft(where, basis, snapshots, jobs, after=()):
    n, cells = len(jobs), sum(width for _, _, width in jobs)
    return pl.pallas_call(
        functools.partial(dft_kernel, jobs, len(after)),
        in_specs=[SMEM_SPACE] + [pl.BlockSpec(memory_space=pl.ANY)] * (2 + len(after)),
        out_specs=[VMEM_SPACE] * n,
        out_shape=[jax.ShapeDtypeStruct((2, 2, 2 * FREQS, width), jnp.bfloat16) for _, _, width in jobs],
        scratch_shapes=[pltpu.VMEM((2, 2, SNAPS, width), jnp.bfloat16) for _, _, width in jobs]
        + [pltpu.VMEM((2 * FREQS, SNAPS), jnp.bfloat16), pltpu.SemaphoreType.DMA((n + 1,))],
        compiler_params=pltpu.CompilerParams(vmem_limit_bytes=DFT_VMEM),
        cost_estimate=pl.CostEstimate(
            flops=2 * 4 * 2 * FREQS * SNAPS * cells, bytes_accessed=4 * SNAPS * 2 * cells, transcendentals=0
        ),
    )(where, basis, snapshots, *after)


def triad_kernel(start, width, last, where_ref, pairs_ref, places_ref, spans_ref, p0, p1, p2, p3, w_ref, *refs):
    if last:
        before, out_ref, cf, part, left_a, left_b, full_a, full_b, acc = refs
    else:
        acc, cf, part, left_a, left_b, full_a, full_b = refs
    vx = 2 * width
    tiles = vx // 128
    me = where_ref[0]
    for s, piece in enumerate((p0, p1, p2, p3)):
        group = lax.rem(me + N_REAL - s, N_REAL)
        for r in range(2):
            for v in range(2):
                for q in range(width // 128):
                    cf[v * (width // 128) + q, pl.ds(2 * group + r, 2 * FREQS, stride=REALS), :] = piece[
                        r, v, :, q * 128 : (q + 1) * 128
                    ].astype(jnp.float32)
    weights = [
        w_ref[:, pl.ds(pl.multiple_of(me * XQ + start + q * 128, 128), 128)].astype(jnp.float32)
        for q in range(width // 128)
    ]
    weights = [jnp.broadcast_to(weight, (REALS, 128)) for weight in weights]

    def prepare(m, carry):
        re = pl.ds(pl.multiple_of(m * REALS, REALS), REALS)
        im = pl.ds(pl.multiple_of((m + FREQS) * REALS, REALS), REALS)
        rows = pl.ds(pl.multiple_of(m * 2 * REALS, 2 * REALS), 2 * REALS)
        for q in range(tiles):
            a, b = cf[q, re, :], cf[q, im, :]
            part[rows, q * 128 : (q + 1) * 128] = jnp.concatenate([a, b], axis=0).astype(jnp.bfloat16)
            part[rows, vx + q * 128 : vx + (q + 1) * 128] = jnp.concatenate([b, -a], axis=0).astype(jnp.bfloat16)
        return carry

    lax.fori_loop(0, FREQS, prepare, 0, unroll=4)
    acc[...] = jnp.zeros_like(acc)
    lane_group = lax.broadcasted_iota(jnp.int32, (REALS, 128), 1) // (2 * REALS)

    def build(left, block):
        for pair in range(TB // 2):
            rows = slice(2 * REALS * pair, 2 * REALS * (pair + 1))
            slices = []
            for h in range(2):
                word = pairs_ref[block * TB + 2 * pair + h]
                slices.append([pl.ds(pl.multiple_of(n, 2 * REALS), 2 * REALS) for n in (word & 1023, word >> 10)])
            for q in range(tiles):
                lanes = slice(q * 128, (q + 1) * 128)
                weight = weights[q % (width // 128)]
                reals, imags = [], []
                for kr, lr in slices:
                    k, l = part[kr, lanes].astype(jnp.float32), part[lr, lanes].astype(jnp.float32)
                    ak, bk, al, bl = k[:REALS], k[REALS:], l[:REALS], l[REALS:]
                    reals.append((ak * al - bk * bl) * weight)
                    imags.append((ak * bl + bk * al) * weight)
                left[rows, lanes] = jnp.concatenate(reals, axis=0).astype(jnp.bfloat16)
                left[rows, vx + q * 128 : vx + (q + 1) * 128] = jnp.concatenate(imags, axis=0).astype(jnp.bfloat16)

    def multiply(left, full, first, win=WIN):
        rows = pl.ds(pl.multiple_of(first * 2 * REALS, 2 * REALS), win * 2 * REALS)
        prod = lax.dot_general(
            left[...], part[rows, :], (((1,), (1,)), ((), ())), preferred_element_type=jnp.float32
        )
        for c in range(win // 8):
            full[c] = prod[:, c * 128 : (c + 1) * 128]

    def put(full, i, row, half, turn, want):
        tile = pltpu.roll(full[half, pl.ds(i * REALS, REALS), :], turn, 1)
        pltpu.store(acc.at[pl.ds(pl.multiple_of(row, REALS), REALS), :], tile, mask=lane_group == want)

    def extract(full, block):
        for i in range(TB):
            word = places_ref[block * TB + i]
            put(full, i, word & 1016, (word >> 10) & 3, (word >> 8) & 112, word >> 15)

    blocks = TRIADS // TB
    build(left_a, 0)
    multiply(left_a, full_a, spans_ref[0], WIN_FIRST)
    build(left_b, 1)

    def stage(left, full, block, left_next, full_last):
        multiply(left, full, spans_ref[block])
        build(left_next, jnp.minimum(block + 1, blocks - 1))
        extract(full_last, block - 1)

    def step(i, carry):
        stage(left_b, full_b, 2 * i + 1, left_a, full_a)
        stage(left_a, full_a, 2 * i + 2, left_b, full_b)
        return carry

    lax.fori_loop(0, blocks // 2 - 1, step, 0)
    stage(left_b, full_b, blocks - 1, left_a, full_a)
    extract(full_b, blocks - 1)

    def beyond(block, carry):
        high = spans_ref[blocks + block]

        def more(first):
            low = jnp.minimum(first, FREQS - WIN)
            build(left_a, block)
            multiply(left_a, full_a, low)

            def one(i, carry):
                pair, slot = pairs_ref[block * TB + i], places_ref[block * TB + i] & 1023
                at = ((pair & 1023) + (pair >> 10)) // (2 * REALS) - low
                inside = jnp.logical_and(at >= 0, at < WIN)
                at = at & (WIN - 1)
                turn = ((slot - at) & 7) * (2 * REALS)
                put(full_a, i, slot & 1016, at >> 3, turn, jnp.where(inside, slot & 7, -1))
                return carry

            lax.fori_loop(0, TB, one, 0)
            return first + WIN

        lax.while_loop(lambda first: first <= high, more, spans_ref[block] + jnp.where(block == 0, WIN_FIRST, WIN))
        return carry

    @pl.when(spans_ref[2 * blocks] > 0)
    def _():
        lax.fori_loop(0, blocks, beyond, 0)


    if last:
        own = w_ref[:, pl.ds(pl.multiple_of(me * XQ, 128), XQ)].astype(jnp.float32)
        square = jnp.broadcast_to(jnp.sum(own * own, axis=1, keepdims=True), (1, 128))
        for o in range(N_CELL):
            for y in range(N_REAL):
                to = ROWS * (o * N_REAL + y)
                for r in range(2):
                    rows = pl.ds(o * OWN_MOST + 2 * y + r, 4, stride=REALS)
                    out_ref[to + 4 * r : to + 4 * r + 4, :] = acc[rows, :] + before[rows, :]
                out_ref[to + 8 : to + 9, :] = square


def triads(where, plan, pieces, quad_weights, start, width, before=None):
    vx, last = 2 * width, before is not None
    sums = jax.ShapeDtypeStruct((N_CELL * OWN_MOST, 128), jnp.float32)
    sent = jax.ShapeDtypeStruct((N_CELL * N_REAL * ROWS, 128), jnp.float32)
    return pl.pallas_call(
        functools.partial(triad_kernel, start, width, last),
        in_specs=[SMEM_SPACE] * 4 + [VMEM_SPACE] * (6 if last else 5),
        out_specs=VMEM_SPACE,
        scratch_shapes=[
            pltpu.VMEM((vx // 128, 2 * FREQS * REALS, 128), jnp.float32),
            pltpu.VMEM((2 * FREQS * REALS, 2 * vx), jnp.bfloat16),
            pltpu.VMEM((TB * REALS, 2 * vx), jnp.bfloat16),
            pltpu.VMEM((TB * REALS, 2 * vx), jnp.bfloat16),
            pltpu.VMEM((WIN_FIRST // 8, TB * REALS, 128), jnp.float32),
            pltpu.VMEM((WIN_FIRST // 8, TB * REALS, 128), jnp.float32),
        ]
        + ([pltpu.VMEM(sums.shape, jnp.float32)] if last else []),
        out_shape=sent if last else sums,
        compiler_params=pltpu.CompilerParams(vmem_limit_bytes=24 * 1024 * 1024),
        cost_estimate=pl.CostEstimate(flops=20_000_000 * width, bytes_accessed=2 * 1024 * 1024, transcendentals=0),
    )(where, *plan, *pieces, quad_weights, *([before] if last else []))


def finish_kernel(received_ref, out_ref, sums):
    period = 8 * ROWS
    total = received_ref[0:period, :]
    for i in range(1, N_CELL * N_REAL * ROWS // period):
        total = total + received_ref[i * period : (i + 1) * period, :]
    sums[...] = total
    rows = [jnp.sum(sums[pl.ds(r, 8, stride=ROWS), :], axis=0, keepdims=True) for r in range(ROWS)]
    scale = 1.0 / jnp.sqrt(rows[8])
    values = jnp.concatenate([row * scale for row in rows[:8]], axis=0)
    turned = jnp.concatenate([values, jnp.zeros((120, 128), jnp.float32)], axis=0).T
    lane = lax.broadcasted_iota(jnp.int32, (2 * REALS, 128), 1)
    for i in range(2):
        placed = jnp.zeros((2 * REALS, 128), jnp.float32)
        for t in range(8):
            piece = turned[t * 2 * REALS : (t + 1) * 2 * REALS, :]
            placed = jnp.where(lane // 4 == t, pltpu.roll(piece, (4 * t - 4 * i) % 128, 1), placed)
        for c in range(2):
            for j in range(REALS):
                out_ref[i, j, c : c + 1, :] = placed[c * REALS + j : c * REALS + j + 1, :OWN_MOST]


def finish(received):
    return pl.pallas_call(
        finish_kernel,
        in_specs=[VMEM_SPACE],
        out_specs=VMEM_SPACE,
        scratch_shapes=[pltpu.VMEM((8 * ROWS, 128), jnp.float32)],
        out_shape=jax.ShapeDtypeStruct((2, REALS, 2, OWN_MOST), jnp.float32),
        compiler_params=pltpu.CompilerParams(vmem_limit_bytes=4 * 1024 * 1024),
    )(received)


def triad_plan(triad_pairs, owner_counts):
    ids = jnp.arange(TRIADS, dtype=jnp.int32)
    owners = jnp.arange(N_CELL, dtype=jnp.int32)
    ending = jnp.sum(jnp.where(owners[None, :] <= owners[:, None], owner_counts[None, :], 0), axis=1)
    past = ids[:, None] >= ending[None, :]
    owner = jnp.sum(past.astype(jnp.int32), axis=1)
    start = jnp.sum(jnp.where(past, owner_counts[None, :], 0), axis=1)
    place = ids - start
    slot = owner * OWN_MOST + (place & 3) * 8 + (place >> 2)
    first, second = triad_pairs[:, 0], triad_pairs[:, 1]
    key = (first + second) * TRIADS + ids
    rank = jnp.sum((key[None, :] < key[:, None]).astype(jnp.int32), axis=1)
    word = first + second * FREQS + slot * FREQS * FREQS
    word = jnp.sum(jnp.where(rank[None, :] == ids[:, None], word[None, :], 0), axis=1)
    first, second, slot = word & 63, (word >> 6) & 63, word >> 12
    total = (first + second).reshape(-1, TB)
    win = jnp.where(jnp.arange(TRIADS // TB) == 0, WIN_FIRST, WIN)
    low, high = jnp.minimum(total[:, 0], FREQS - win), total[:, TB - 1]
    at = (total - low[:, None]).reshape(-1)
    outside = ((total - low[:, None]) >= win[:, None]).reshape(-1).astype(jnp.int32)
    turn = (slot - at) & 7
    places = slot + (((at >> 3) & 3) << 10) + (turn << 12) + (((slot & 7) + 8 * outside) << 15)
    pairs = first * 2 * REALS + ((second * 2 * REALS) << 10)
    return pairs, places, jnp.concatenate([low, high, jnp.max(outside, keepdims=True)])


def local(snapshots, quad_weights, triad_pairs, owner_counts):
    basis = dft_table()
    where = lax.axis_index("real").astype(jnp.int32).reshape(1)
    weights = quad_weights.reshape(1, -1)
    shifts = (1, 3, 2)
    (first, width), (second, width2) = PARTS
    early = tuple((s, first, width) for s in shifts) + ((0, first, width), (0, second, width2))
    early = dft(where, basis, snapshots, early)
    late = dft(where, basis, snapshots, tuple((s, second, width2) for s in shifts), (early[0],))
    away, own = [early[:3], late], early[3:]
    arrived = []
    for pieces in away:
        moved = [
            lax.ppermute(piece, "real", [(i, (i + s) % N_REAL) for i in range(N_REAL)])
            for piece, s in zip(pieces, shifts)
        ]
        arrived.append((moved[0], moved[2], moved[1]))
    later_pairs, ready = lax.optimization_barrier((triad_pairs, arrived[0][1]))
    arrived[0] = (arrived[0][0], ready, arrived[0][2])
    plan = triad_plan(later_pairs, owner_counts)
    sums = None
    for (start, width), pieces, here in zip(PARTS, arrived, own):
        sums = triads(where, plan, (here,) + pieces, weights, start, width, sums)
    sums = sums.reshape(N_CELL * N_REAL, 1, ROWS * 128)
    received = lax.all_to_all(sums, ("cell", "real"), split_axis=0, concat_axis=0, tiled=True)
    values = finish(received.reshape(N_CELL * N_REAL * ROWS, 128))
    return jnp.transpose(values, (3, 0, 1, 2))


def solution(mesh):
    return jax.shard_map(
        local,
        mesh=mesh,
        in_specs=(P("real", None, None, "cell"), P("cell"), P(), P()),
        out_specs=P("cell", "real", None, None),
        check_vma=False,
    )
```

```python
import functools

import jax
import jax.numpy as jnp
import numpy as np
from jax import lax
from jax.experimental import pallas as pl
from jax.experimental.pallas import tpu as pltpu
from jax.sharding import PartitionSpec as P

SNAPS = 256
FREQS = 64
REALS = 8
TRIADS = 512
OWN_MOST = 32
N_REAL = 4
N_CELL = 32
XQ = 512
PARTS = ((0, 256), (256, 256))
TB = 64
WIN = 16
WIN_FIRST = 32
ROWS = 9
DFT_VMEM = 115 * 512 * 1024
VMEM_SPACE = pl.BlockSpec(memory_space=pltpu.VMEM)
SMEM_SPACE = pl.BlockSpec(memory_space=pltpu.SMEM)


def dft_table():
    times = np.arange(SNAPS)
    bins = np.arange(FREQS)
    window = 0.5 - 0.5 * np.cos(2.0 * np.pi * times / SNAPS)
    norm = np.sqrt(np.sum(window * window))
    phases = 2.0 * np.pi * ((bins[:, None] * times[None, :]) % SNAPS) / SNAPS
    table = np.concatenate([window * np.cos(phases), -window * np.sin(phases)], axis=0) / norm
    return jnp.asarray(table.astype(np.float32)).astype(jnp.bfloat16)


def dft_kernel(jobs, after, where_ref, basis_ref, snapshots_ref, *refs):
    n, refs = len(jobs), refs[after:]
    outs, bufs, basis, sems = refs[:n], refs[n : 2 * n], refs[2 * n], refs[2 * n + 1]
    table = pltpu.make_async_copy(basis_ref, basis, sems.at[n])
    table.start()
    copies = []
    for i, (s, start, width) in enumerate(jobs):
        at = pl.multiple_of(lax.rem(where_ref[0] + s, N_REAL) * XQ + start, 128)
        copies.append(
            pltpu.make_async_copy(snapshots_ref.at[:, :, :, pl.ds(at, width)], bufs[i], sems.at[i])
        )
        copies[-1].start()
    table.wait()
    for i in range(n):
        copies[i].wait()
        for r in range(2):
            for v in range(2):
                outs[i][r, v] = jnp.dot(
                    basis[...], bufs[i][r, v], preferred_element_type=jnp.float32
                ).astype(jnp.bfloat16)


def dft(where, basis, snapshots, jobs, after=()):
    n, cells = len(jobs), sum(width for _, _, width in jobs)
    return pl.pallas_call(
        functools.partial(dft_kernel, jobs, len(after)),
        in_specs=[SMEM_SPACE] + [pl.BlockSpec(memory_space=pl.ANY)] * (2 + len(after)),
        out_specs=[VMEM_SPACE] * n,
        out_shape=[jax.ShapeDtypeStruct((2, 2, 2 * FREQS, width), jnp.bfloat16) for _, _, width in jobs],
        scratch_shapes=[pltpu.VMEM((2, 2, SNAPS, width), jnp.bfloat16) for _, _, width in jobs]
        + [pltpu.VMEM((2 * FREQS, SNAPS), jnp.bfloat16), pltpu.SemaphoreType.DMA((n + 1,))],
        compiler_params=pltpu.CompilerParams(vmem_limit_bytes=DFT_VMEM),
        cost_estimate=pl.CostEstimate(
            flops=2 * 4 * 2 * FREQS * SNAPS * cells, bytes_accessed=4 * SNAPS * 2 * cells, transcendentals=0
        ),
    )(where, basis, snapshots, *after)


def triad_kernel(start, width, last, where_ref, pairs_ref, places_ref, spans_ref, p0, p1, p2, p3, w_ref, *refs):
    if last:
        before, out_ref, cf, part, left_a, left_b, full_a, full_b, acc = refs
    else:
        acc, cf, part, left_a, left_b, full_a, full_b = refs
    vx = 2 * width
    tiles = vx // 128
    me = where_ref[0]
    for s, piece in enumerate((p0, p1, p2, p3)):
        group = lax.rem(me + N_REAL - s, N_REAL)
        for r in range(2):
            for v in range(2):
                for q in range(width // 128):
                    cf[v * (width // 128) + q, pl.ds(2 * group + r, 2 * FREQS, stride=REALS), :] = piece[
                        r, v, :, q * 128 : (q + 1) * 128
                    ].astype(jnp.float32)
    weights = [
        w_ref[:, pl.ds(pl.multiple_of(me * XQ + start + q * 128, 128), 128)].astype(jnp.float32)
        for q in range(width // 128)
    ]
    weights = [jnp.broadcast_to(weight, (REALS, 128)) for weight in weights]

    def prepare(m, carry):
        re = pl.ds(pl.multiple_of(m * REALS, REALS), REALS)
        im = pl.ds(pl.multiple_of((m + FREQS) * REALS, REALS), REALS)
        rows = pl.ds(pl.multiple_of(m * 2 * REALS, 2 * REALS), 2 * REALS)
        for q in range(tiles):
            a, b = cf[q, re, :], cf[q, im, :]
            part[rows, q * 128 : (q + 1) * 128] = jnp.concatenate([a, b], axis=0).astype(jnp.bfloat16)
            part[rows, vx + q * 128 : vx + (q + 1) * 128] = jnp.concatenate([b, -a], axis=0).astype(jnp.bfloat16)
        return carry

    lax.fori_loop(0, FREQS, prepare, 0, unroll=4)
    acc[...] = jnp.zeros_like(acc)
    lane_group = lax.broadcasted_iota(jnp.int32, (REALS, 128), 1) // (2 * REALS)

    def build(left, block):
        for pair in range(TB // 2):
            rows = slice(2 * REALS * pair, 2 * REALS * (pair + 1))
            slices = []
            for h in range(2):
                word = pairs_ref[block * TB + 2 * pair + h]
                slices.append([pl.ds(pl.multiple_of(n, 2 * REALS), 2 * REALS) for n in (word & 1023, word >> 10)])
            for q in range(tiles):
                lanes = slice(q * 128, (q + 1) * 128)
                weight = weights[q % (width // 128)]
                reals, imags = [], []
                for kr, lr in slices:
                    k, l = part[kr, lanes].astype(jnp.float32), part[lr, lanes].astype(jnp.float32)
                    ak, bk, al, bl = k[:REALS], k[REALS:], l[:REALS], l[REALS:]
                    reals.append((ak * al - bk * bl) * weight)
                    imags.append((ak * bl + bk * al) * weight)
                left[rows, lanes] = jnp.concatenate(reals, axis=0).astype(jnp.bfloat16)
                left[rows, vx + q * 128 : vx + (q + 1) * 128] = jnp.concatenate(imags, axis=0).astype(jnp.bfloat16)

    def multiply(left, full, first, win=WIN):
        rows = pl.ds(pl.multiple_of(first * 2 * REALS, 2 * REALS), win * 2 * REALS)
        prod = lax.dot_general(
            left[...], part[rows, :], (((1,), (1,)), ((), ())), preferred_element_type=jnp.float32
        )
        for c in range(win // 8):
            full[c] = prod[:, c * 128 : (c + 1) * 128]

    def put(full, i, row, half, turn, want):
        tile = pltpu.roll(full[half, pl.ds(i * REALS, REALS), :], turn, 1)
        pltpu.store(acc.at[pl.ds(pl.multiple_of(row, REALS), REALS), :], tile, mask=lane_group == want)

    def extract(full, block):
        for i in range(TB):
            word = places_ref[block * TB + i]
            put(full, i, word & 1016, (word >> 10) & 3, (word >> 8) & 112, word >> 15)

    blocks = TRIADS // TB
    build(left_a, 0)
    multiply(left_a, full_a, spans_ref[0], WIN_FIRST)
    build(left_b, 1)

    def stage(left, full, block, left_next, full_last):
        multiply(left, full, spans_ref[block])
        build(left_next, jnp.minimum(block + 1, blocks - 1))
        extract(full_last, block - 1)

    def step(i, carry):
        stage(left_b, full_b, 2 * i + 1, left_a, full_a)
        stage(left_a, full_a, 2 * i + 2, left_b, full_b)
        return carry

    lax.fori_loop(0, blocks // 2 - 1, step, 0)
    stage(left_b, full_b, blocks - 1, left_a, full_a)
    extract(full_b, blocks - 1)

    def beyond(block, carry):
        high = spans_ref[blocks + block]

        def more(first):
            low = jnp.minimum(first, FREQS - WIN)
            build(left_a, block)
            multiply(left_a, full_a, low)

            def one(i, carry):
                pair, slot = pairs_ref[block * TB + i], places_ref[block * TB + i] & 1023
                at = ((pair & 1023) + (pair >> 10)) // (2 * REALS) - low
                inside = jnp.logical_and(at >= 0, at < WIN)
                at = at & (WIN - 1)
                turn = ((slot - at) & 7) * (2 * REALS)
                put(full_a, i, slot & 1016, at >> 3, turn, jnp.where(inside, slot & 7, -1))
                return carry

            lax.fori_loop(0, TB, one, 0)
            return first + WIN

        lax.while_loop(lambda first: first <= high, more, spans_ref[block] + jnp.where(block == 0, WIN_FIRST, WIN))
        return carry

    lax.fori_loop(0, blocks, beyond, 0)

    if last:
        own = w_ref[:, pl.ds(pl.multiple_of(me * XQ, 128), XQ)].astype(jnp.float32)
        square = jnp.broadcast_to(jnp.sum(own * own, axis=1, keepdims=True), (1, 128))
        for o in range(N_CELL):
            for y in range(N_REAL):
                to = ROWS * (y * N_CELL + o)
                for r in range(2):
                    rows = pl.ds(o * OWN_MOST + 2 * y + r, 4, stride=REALS)
                    out_ref[to + 4 * r : to + 4 * r + 4, :] = acc[rows, :] + before[rows, :]
                out_ref[to + 8 : to + 9, :] = square


def triads(where, plan, pieces, quad_weights, start, width, before=None):
    vx, last = 2 * width, before is not None
    sums = jax.ShapeDtypeStruct((N_CELL * OWN_MOST, 128), jnp.float32)
    sent = jax.ShapeDtypeStruct((N_CELL * N_REAL * ROWS, 128), jnp.float32)
    return pl.pallas_call(
        functools.partial(triad_kernel, start, width, last),
        in_specs=[SMEM_SPACE] * 4 + [VMEM_SPACE] * (6 if last else 5),
        out_specs=VMEM_SPACE,
        scratch_shapes=[
            pltpu.VMEM((vx // 128, 2 * FREQS * REALS, 128), jnp.float32),
            pltpu.VMEM((2 * FREQS * REALS, 2 * vx), jnp.bfloat16),
            pltpu.VMEM((TB * REALS, 2 * vx), jnp.bfloat16),
            pltpu.VMEM((TB * REALS, 2 * vx), jnp.bfloat16),
            pltpu.VMEM((WIN_FIRST // 8, TB * REALS, 128), jnp.float32),
            pltpu.VMEM((WIN_FIRST // 8, TB * REALS, 128), jnp.float32),
        ]
        + ([pltpu.VMEM(sums.shape, jnp.float32)] if last else []),
        out_shape=sent if last else sums,
        compiler_params=pltpu.CompilerParams(vmem_limit_bytes=24 * 1024 * 1024),
        cost_estimate=pl.CostEstimate(flops=20_000_000 * width, bytes_accessed=2 * 1024 * 1024, transcendentals=0),
    )(where, *plan, *pieces, quad_weights, *([before] if last else []))


def finish_kernel(received_ref, out_ref, sums):
    period = 8 * ROWS
    total = received_ref[0:period, :]
    for i in range(1, N_CELL * N_REAL * ROWS // period):
        total = total + received_ref[i * period : (i + 1) * period, :]
    sums[...] = total
    rows = [jnp.sum(sums[pl.ds(r, 8, stride=ROWS), :], axis=0, keepdims=True) for r in range(ROWS)]
    scale = 1.0 / jnp.sqrt(rows[8])
    values = jnp.concatenate([row * scale for row in rows[:8]], axis=0)
    turned = jnp.concatenate([values, jnp.zeros((120, 128), jnp.float32)], axis=0).T
    lane = lax.broadcasted_iota(jnp.int32, (2 * REALS, 128), 1)
    for i in range(2):
        placed = jnp.zeros((2 * REALS, 128), jnp.float32)
        for t in range(8):
            piece = turned[t * 2 * REALS : (t + 1) * 2 * REALS, :]
            placed = jnp.where(lane // 4 == t, pltpu.roll(piece, (4 * t - 4 * i) % 128, 1), placed)
        for c in range(2):
            for j in range(REALS):
                out_ref[i, j, c : c + 1, :] = placed[c * REALS + j : c * REALS + j + 1, :OWN_MOST]


def finish(received):
    return pl.pallas_call(
        finish_kernel,
        in_specs=[VMEM_SPACE],
        out_specs=VMEM_SPACE,
        scratch_shapes=[pltpu.VMEM((8 * ROWS, 128), jnp.float32)],
        out_shape=jax.ShapeDtypeStruct((2, REALS, 2, OWN_MOST), jnp.float32),
        compiler_params=pltpu.CompilerParams(vmem_limit_bytes=4 * 1024 * 1024),
    )(received)


def triad_plan(triad_pairs, owner_counts):
    ids = jnp.arange(TRIADS, dtype=jnp.int32)
    owners = jnp.arange(N_CELL, dtype=jnp.int32)
    ending = jnp.sum(jnp.where(owners[None, :] <= owners[:, None], owner_counts[None, :], 0), axis=1)
    past = ids[:, None] >= ending[None, :]
    owner = jnp.sum(past.astype(jnp.int32), axis=1)
    start = jnp.sum(jnp.where(past, owner_counts[None, :], 0), axis=1)
    place = ids - start
    slot = owner * OWN_MOST + (place & 3) * 8 + (place >> 2)
    first, second = triad_pairs[:, 0], triad_pairs[:, 1]
    key = (first + second) * TRIADS + ids
    rank = jnp.sum((key[None, :] < key[:, None]).astype(jnp.int32), axis=1)
    word = first + second * FREQS + slot * FREQS * FREQS
    word = jnp.sum(jnp.where(rank[None, :] == ids[:, None], word[None, :], 0), axis=1)
    first, second, slot = word & 63, (word >> 6) & 63, word >> 12
    total = (first + second).reshape(-1, TB)
    win = jnp.where(jnp.arange(TRIADS // TB) == 0, WIN_FIRST, WIN)
    low, high = jnp.minimum(total[:, 0], FREQS - win), total[:, TB - 1]
    at = (total - low[:, None]).reshape(-1)
    outside = ((total - low[:, None]) >= win[:, None]).reshape(-1).astype(jnp.int32)
    turn = (slot - at) & 7
    places = slot + (((at >> 3) & 3) << 10) + (turn << 12) + (((slot & 7) + 8 * outside) << 15)
    pairs = first * 2 * REALS + ((second * 2 * REALS) << 10)
    return pairs, places, jnp.concatenate([low, high])


def local(snapshots, quad_weights, triad_pairs, owner_counts):
    basis = dft_table()
    where = lax.axis_index("real").astype(jnp.int32).reshape(1)
    weights = quad_weights.reshape(1, -1)
    plan = triad_plan(triad_pairs, owner_counts)
    shifts = (1, 3, 2)
    (first, width), (second, width2) = PARTS
    early = tuple((s, first, width) for s in shifts) + ((0, first, width), (0, second, width2))
    early = dft(where, basis, snapshots, early)
    late = dft(where, basis, snapshots, tuple((s, second, width2) for s in shifts), (early[0],))
    away, own = [early[:3], late], early[3:]
    arrived = []
    for pieces in away:
        moved = [
            lax.ppermute(piece, "real", [(i, (i + s) % N_REAL) for i in range(N_REAL)])
            for piece, s in zip(pieces, shifts)
        ]
        arrived.append((moved[0], moved[2], moved[1]))
    sums = None
    for (start, width), pieces, here in zip(PARTS, arrived, own):
        sums = triads(where, plan, (here,) + pieces, weights, start, width, sums)
    sums = sums.reshape(N_CELL * N_REAL, 1, ROWS * 128)
    received = lax.all_to_all(sums, ("real", "cell"), split_axis=0, concat_axis=0, tiled=True)
    values = finish(received.reshape(N_CELL * N_REAL * ROWS, 128))
    return jnp.transpose(values, (3, 0, 1, 2))


def solution(mesh):
    return jax.shard_map(
        local,
        mesh=mesh,
        in_specs=(P("real", None, None, "cell"), P("cell"), P(), P()),
        out_specs=P("cell", "real", None, None),
        check_vma=False,
    )
```
